128 devices in a mesh: ctx: 8 (over x, y_lo), exp: 16 (over y_hi, z, core).
Axes of the slice: x: 4, y: 4 (y_hi: 2, y_lo: 2; y = y_hi * 2 + y_lo), z: 4, core: 2. Of those that a mesh axis runs over, the one named last changes fastest.
Arguments:
- queries: bfloat16 [2048, 4096], P('ctx', 'exp'), may hold values from -4.5 to 4.5, as said below
- keys: bfloat16 [2048, 512], P('ctx'), may hold values from -4.5 to 4.5, as said below
- values: bfloat16 [2048, 512], P('ctx'), may hold values from -6 to 6
- out_proj: bfloat16 [4096, 4096], P('exp'), may hold values from -0.5 to 0.5
- residual: bfloat16 [2048, 4096], P(('ctx', 'exp')), may hold values from -3 to 3
- norm_gain: float32 [4096], replicated, may hold values from 0.5 to 1.5
- routes: int32 [2048, 8], P(('ctx', 'exp')), may hold values from 0 to 127, all different within a row; in each aligned block of 16 rows (0 to 15, 16 to 31, ...) at most 2 rows name the same one
- route_weights: float32 [2048, 8], P(('ctx', 'exp')), may hold values from 0.2 to 1
- w_gate: bfloat16 [128, 4096, 768], P(('ctx', 'exp')), may hold values from -0.09375 to 0.09375
- w_up: bfloat16 [128, 4096, 768], P(('ctx', 'exp')), may hold values from -0.09375 to 0.09375
- w_down: bfloat16 [128, 768, 4096], P(('ctx', 'exp')), may hold values from -0.21875 to 0.21875
Outputs:
- hidden_state: bfloat16 [2048, 4096], P(('ctx', 'exp'))
- expert_mix: float32 [2048, 4096], P(('ctx', 'exp'))
The draws below stay inside these ranges and needn't reach their ends.
Inputs may be any that keep to these rules, and one draw needn't show every extreme that they name: Entries of queries are real values within the range. Entries of keys are real values within the range. `routes`: each token names 8 different experts; the 16 tokens of one device (aligned blocks of rows) name any one expert at most 2 times, a bound that some block reaches.
All inputs are finite; a program needn't handle non-finite values.
Results may differ from the reference program's by a relative error of at most 0.03.
Values may be sent and summed in bfloat16 or wider, within the bound.
No kernel may reach another device: no remote copies, remote signals or barrier semaphores. Data moves between devices by JAX's collectives and lax.ppermute only.
A program may use at most 128 MiB of HBM per device.

```python
import math
import jax
import jax.numpy as jnp
import numpy as np
from jax import lax

D = 4096
QUERY_HEADS = 32
KEY_VALUE_HEADS = 4
HEAD_WIDTH = 128
FF = 768
TOP = 8
SEQUENCE_LENGTH = 2048
TOK_MOE = 16
EXPERTS = 128
CAP = 2
N_CTX = 8
N_EXP = 16


def draw_queries(key, part):
    key = jax.random.fold_in(key, 11)
    return jnp.clip(jax.random.normal(key, (SEQUENCE_LENGTH, QUERY_HEADS * HEAD_WIDTH), jnp.float32), -4.5, 4.5).astype(jnp.bfloat16)


def draw_keys(key, part):
    key = jax.random.fold_in(key, 12)
    return jnp.clip(jax.random.normal(key, (SEQUENCE_LENGTH, KEY_VALUE_HEADS * HEAD_WIDTH), jnp.float32), -4.5, 4.5).astype(jnp.bfloat16)


def block_levels(own_key, dims, cuts, low, largest):
    def one(dim, blocks):
        draws = jax.random.uniform(jax.random.fold_in(jax.random.fold_in(own_key, 6), dim), (blocks,), jnp.float32, low / len(cuts), largest / len(cuts))
        return jnp.repeat(jnp.exp(draws), dims[dim] // blocks).reshape((-1,) + (1,) * (len(dims) - dim - 1))

    level = one(*cuts[0])
    for cut in cuts[1:]:
        level = level * one(*cut)
    return level


def shared_out(own_key, own, number, rows, number_of, top, reach, lean):
    order = jax.random.permutation(own_key, number_of)
    heavy_load, ordinary = load_shares(number_of, rows * top, reach, lean, True), load_shares(number_of, rows * top, reach, lean, False)
    places = jnp.arange(number_of)

    def named(lengths, rotation):
        used = int((lengths > 0).sum())
        fixed = max(1, used // 4)
        passed = fixed + (places - fixed + rotation * (used - fixed)) % max(1, number_of - fixed)
        return jnp.zeros((number_of,), jnp.int32).at[order[jnp.where(places < fixed, places, passed)]].set(jnp.asarray(lengths, jnp.int32))

    lengths = jnp.where(number % 4 == 0, named(heavy_load, number // 4), named(ordinary, number - number // 4 - 1))
    mixed = jax.random.permutation(jax.random.fold_in(own, 3), number_of)
    donor, sink = mixed[0:number_of // 2 * 2:2], mixed[1:number_of // 2 * 2:2]
    margin = jnp.minimum(lengths[donor] - 1, reach - lengths[sink]) // 2
    margin = jnp.where((donor == order[0]) | (sink == order[0]) | (lengths[sink] == 0), 0, jnp.maximum(margin, 0))
    passed = jax.random.randint(jax.random.fold_in(own, 4), (number_of // 2,), 0, 1 << 20) % (margin + 1)
    lengths = lengths.at[donor].add(-passed).at[sink].add(passed)
    labels = jnp.searchsorted(jnp.cumsum(lengths), jnp.arange(rows * top), side="right").astype(jnp.int32)
    grid = labels.reshape(top, rows).T
    grid = grid[jax.random.permutation(jax.random.fold_in(own, 1), rows)]
    rotation = jax.random.randint(jax.random.fold_in(own, 2), (rows, 1), 0, top)
    return jnp.take_along_axis(grid, (jnp.arange(top)[None, :] + rotation) % top, axis=1)


def load_shares(amount, total, reach, skew, full):
    portions = [(1 << 20) // math.isqrt(standing ** skew) + 1 for standing in range(1, amount + 1)]
    largest = reach if full else min(reach, max(-(-total // amount), total * portions[0] // sum(portions)))
    least = 1 if total - largest >= amount - 1 else 0
    given, spare = [largest] + [least] * (amount - 1), total - largest - least * (amount - 1)
    while spare > 0:
        free = [i for i in range(1, amount) if given[i] < largest] or [i for i in range(1, amount) if given[i] < reach]
        pool, budget = sum([portions[i] for i in free]), spare
        for i in free:
            addition = min(reach - given[i], max(1, budget * portions[i] // pool), spare)
            given[i] = given[i] + addition
            spare = spare - addition
    return np.array(given)


def bell_draw(own_key, dims, spread, reach, split=(), kind=jnp.bfloat16):
    gain = block_levels(own_key, dims, split, -0.22, 0.18) if split else 1.0
    entries = jax.random.normal(own_key, dims, jnp.float32) * spread * gain
    return jnp.minimum(jnp.maximum(entries, -reach), reach).astype(kind)


def setup_inputs(seed: int = 0) -> dict:
    arg_keys = jax.random.split(jax.random.key(seed), 12)
    queries = draw_queries(jax.random.fold_in(arg_keys[11], 71), 0)
    keys = draw_keys(jax.random.fold_in(arg_keys[11], 71), 0)
    values = bell_draw(arg_keys[2], (SEQUENCE_LENGTH, KEY_VALUE_HEADS * HEAD_WIDTH), 1.0, 6.0, ((0, 8),))
    out_proj = bell_draw(arg_keys[3], (QUERY_HEADS * HEAD_WIDTH, D), HEAD_WIDTH ** -0.5, 0.5, ((0, 16),))
    residual = bell_draw(arg_keys[4], (SEQUENCE_LENGTH, D), 0.5, 3.0, ((0, 128),))
    norm_gain = jnp.clip(1.0 + 0.1 * jax.random.normal(arg_keys[5], (D,), jnp.float32), 0.5, 1.5)
    routes_keys = jax.random.split(jax.random.fold_in(arg_keys[6], 1), SEQUENCE_LENGTH // TOK_MOE)
    routes_turns = jax.random.permutation(jax.random.fold_in(arg_keys[6], 3), SEQUENCE_LENGTH // TOK_MOE)
    routes = jax.vmap(lambda own, number: shared_out(jax.random.fold_in(arg_keys[6], 2), own, number, TOK_MOE, EXPERTS, TOP, CAP, 2))(routes_keys, routes_turns).reshape((SEQUENCE_LENGTH, TOP))
    route_weights = jnp.clip(0.2 + 0.8 * jax.random.uniform(arg_keys[7], (SEQUENCE_LENGTH, TOP), jnp.float32) ** block_levels(arg_keys[7], (SEQUENCE_LENGTH, TOP), ((0, 128),), -0.2, 0.2), 0.2, 1.0)
    w_gate = bell_draw(arg_keys[8], (EXPERTS, D, FF), D ** -0.5, 0.09375, ((0, 128),))
    w_up = bell_draw(arg_keys[9], (EXPERTS, D, FF), D ** -0.5, 0.09375, ((0, 128),))
    w_down = bell_draw(arg_keys[10], (EXPERTS, FF, D), FF ** -0.5, 0.21875, ((0, 128),))
    return {"queries": queries, "keys": keys, "values": values, "out_proj": out_proj, "residual": residual, "norm_gain": norm_gain, "routes": routes, "route_weights": route_weights, "w_gate": w_gate, "w_up": w_up, "w_down": w_down}


def expert_rows(row_block, gate_matrix, up_matrix, down_matrix):
    gate = jnp.dot(row_block, gate_matrix, preferred_element_type=jnp.float32)
    upward = jnp.dot(row_block, up_matrix, preferred_element_type=jnp.float32)
    active = (jax.nn.silu(gate) * upward).astype(jnp.bfloat16)
    return jnp.dot(active, down_matrix, preferred_element_type=jnp.float32).astype(jnp.bfloat16)

def reference(queries, keys, values, out_proj, residual, norm_gain, routes, route_weights, w_gate, w_up, w_down):
    heads_per_group = QUERY_HEADS // KEY_VALUE_HEADS
    block_rows = min(512, SEQUENCE_LENGTH)
    block_count = SEQUENCE_LENGTH // block_rows
    inv_root = 1.0 / math.sqrt(HEAD_WIDTH)
    query_heads = queries.reshape(SEQUENCE_LENGTH, QUERY_HEADS, HEAD_WIDTH)
    expanded_keys = keys.reshape(SEQUENCE_LENGTH, KEY_VALUE_HEADS, HEAD_WIDTH)
    expanded_values = values.reshape(SEQUENCE_LENGTH, KEY_VALUE_HEADS, HEAD_WIDTH)
    key_pos = lax.iota(jnp.int32, SEQUENCE_LENGTH)

    def one_head(head):
        shared = head // heads_per_group
        head_keys = jnp.take(expanded_keys, shared, axis=1)
        head_values = jnp.take(expanded_values, shared, axis=1)
        head_queries = jnp.take(query_heads, head, axis=1)

        def one_block(block):
            lower = block * block_rows
            query_block = lax.dynamic_slice_in_dim(head_queries, lower, block_rows, 0)
            scores = jnp.dot(query_block, head_keys.T, preferred_element_type=jnp.float32) * inv_root
            query_pos = lower + lax.iota(jnp.int32, block_rows)
            visible = key_pos[None, :] <= query_pos[:, None]
            row_max = lax.optimization_barrier(jnp.max(jnp.where(visible, scores, -1e+30), axis=1, keepdims=True))
            weights = jnp.where(visible, jnp.exp(scores - row_max), 0.0)
            denominator = lax.optimization_barrier(jnp.sum(weights, axis=1, keepdims=True))
            mixed = jnp.dot(weights.astype(jnp.bfloat16), head_values, preferred_element_type=jnp.float32)
            return (mixed / denominator).astype(jnp.bfloat16)
        return lax.map(one_block, jnp.arange(block_count, dtype=jnp.int32)).reshape(SEQUENCE_LENGTH, HEAD_WIDTH)
    attended = lax.map(one_head, jnp.arange(QUERY_HEADS, dtype=jnp.int32))
    attended = attended.transpose(1, 0, 2).reshape(SEQUENCE_LENGTH, QUERY_HEADS * HEAD_WIDTH)
    projected = jnp.dot(attended, out_proj, preferred_element_type=jnp.float32)
    hidden_state = (residual.astype(jnp.float32) + projected).astype(jnp.bfloat16)
    widened = hidden_state.astype(jnp.float32)
    normed = (widened * lax.rsqrt(lax.optimization_barrier(jnp.mean(widened * widened, axis=-1, keepdims=True)) + 1e-06) * norm_gain).astype(jnp.bfloat16)
    slot_count = N_CTX * N_EXP * CAP
    flat_routes = routes.reshape(-1)
    flat_weights = route_weights.reshape(-1)
    token_of = lax.iota(jnp.int32, SEQUENCE_LENGTH * TOP) // TOP

    def one_expert(running, inputs):
        gate_matrix, up_matrix, down_matrix, expert = inputs
        chosen = flat_routes == expert
        ranking = jnp.cumsum(chosen.astype(jnp.int32)) - 1
        target = jnp.where(chosen, ranking, slot_count).astype(jnp.int32)
        sources = jnp.zeros((slot_count,), jnp.int32).at[target].set(token_of, mode='drop')
        scaled = jnp.zeros((slot_count,), route_weights.dtype).at[target].set(flat_weights, mode='drop')
        produced = expert_rows(normed[sources], gate_matrix, up_matrix, down_matrix)
        running = running.at[sources].add(scaled[:, None] * produced.astype(jnp.float32))
        return (running, None)
    expert_mix, unused = lax.scan(one_expert, jnp.zeros((SEQUENCE_LENGTH, D), jnp.float32), (w_gate, w_up, w_down, jnp.arange(EXPERTS, dtype=jnp.int32)))
    return (hidden_state, expert_mix)
```

```python
import math

import jax
import jax.numpy as jnp
from jax import lax
from jax.experimental import pallas as pl
from jax.experimental.pallas import tpu as pltpu
from jax.sharding import Mesh
from jax.sharding import PartitionSpec as P

D = 4096
HEAD_WIDTH = 128
TOP = 8
TOKENS = 16
EXPERTS = 128
CAP = 2
SLOTS = EXPERTS * CAP
BLOCK = 256
FF = 768
PIECES = D // 128
CTX = ("x", "yl")
CHIPS = ("yh", "z")
ALL = ("x", "yl", "yh", "z", "c")
INV_ROOT = 1.0 / math.sqrt(HEAD_WIDTH)
MIB = 1 << 20

VMEM = pl.BlockSpec(memory_space=pltpu.VMEM)
SMEM = pl.BlockSpec(memory_space=pltpu.SMEM)
HBM = pl.BlockSpec(memory_space=pl.ANY)


def attention_kernel(
    place, own_queries, twin_queries, blocks, own_proj, twin_proj, out, w_buf, sems, m_ref, l_ref, acc
):
    copies = [
        pltpu.make_async_copy(own_proj, w_buf.at[pl.ds(0, 256)], sems.at[0]),
        pltpu.make_async_copy(twin_proj, w_buf.at[pl.ds(256, 256)], sems.at[1]),
    ]
    for copy in copies:
        copy.start()
    own_block = place[0]
    core = place[1]
    stacked = jnp.concatenate(
        [
            own_queries[:, 0:128],
            own_queries[:, 128:256],
            twin_queries[:, 0:128],
            twin_queries[:, 128:256],
        ],
        axis=0,
    )

    def scores_of(block):
        return (
            lax.dot_general(
                stacked,
                blocks[block, :, 0:128],
                (((1,), (1,)), ((), ())),
                preferred_element_type=jnp.float32,
            )
            * INV_ROOT
        )

    row = lax.broadcasted_iota(jnp.int32, (512, BLOCK), 0) % 128
    position = (row // TOKENS) * (2 * TOKENS) + core * TOKENS + row % TOKENS
    visible = lax.broadcasted_iota(jnp.int32, (512, BLOCK), 1) <= position
    scores = jnp.where(visible, scores_of(own_block), -1e30)
    row_max = jnp.max(scores, axis=1, keepdims=True)
    probs = jnp.exp(scores - row_max)
    m_ref[...] = jnp.broadcast_to(row_max, (512, 128))
    l_ref[...] = jnp.broadcast_to(jnp.sum(probs, axis=1, keepdims=True), (512, 128))
    acc[...] = jnp.dot(
        probs.astype(jnp.bfloat16),
        blocks[own_block, :, 128:256],
        preferred_element_type=jnp.float32,
    )

    @pl.loop(0, own_block)
    def earlier(block):
        scores = scores_of(block)
        old_max = m_ref[:, 0:1]
        new_max = jnp.maximum(old_max, jnp.max(scores, axis=1, keepdims=True))
        shrink = jnp.exp(old_max - new_max)
        probs = jnp.exp(scores - new_max)
        m_ref[...] = jnp.broadcast_to(new_max, (512, 128))
        l_ref[...] = l_ref[...] * shrink + jnp.sum(probs, axis=1, keepdims=True)
        acc[...] = acc[...] * shrink + jnp.dot(
            probs.astype(jnp.bfloat16),
            blocks[block, :, 128:256],
            preferred_element_type=jnp.float32,
        )

    attended = (acc[...] / l_ref[...]).astype(jnp.bfloat16)
    wide = jnp.concatenate([attended[h * 128 : (h + 1) * 128] for h in range(4)], axis=1)
    for copy in copies:
        copy.wait()

    for piece in range(D // 512):
        columns = slice(piece * 512, (piece + 1) * 512)
        out[:, columns] = jnp.dot(
            wide, w_buf[:, columns], preferred_element_type=jnp.float32
        ).astype(jnp.bfloat16)


def slots_kernel(routes, slots, counts):
    @pl.loop(0, EXPERTS)
    def clear(expert):
        counts[expert] = 0

    @pl.loop(0, TOKENS)
    def number(token):
        for choice in range(TOP):
            expert = routes[token, choice]
            rank = counts[expert]
            counts[expert] = rank + 1
            slots[token, choice] = expert * CAP + rank


def norm_kernel(slots, shares, residual, gain, hidden, outgoing, rows):
    total = residual[...].astype(jnp.float32)
    for share in range(8):
        total = total + shares[share].astype(jnp.float32)
    state = total.astype(jnp.bfloat16)
    hidden[...] = state
    wide = state.astype(jnp.float32)
    scale = lax.rsqrt(jnp.mean(wide * wide, axis=1, keepdims=True) + 1e-6)
    normed = wide * scale * gain[...]
    for piece in range(PIECES):
        rows[pl.ds(piece, TOKENS, stride=PIECES), :] = normed[:, piece * 128 : (piece + 1) * 128]

    @pl.loop(0, SLOTS // 8)
    def clear(group):
        outgoing[pl.ds(group * 8, 8)] = jnp.zeros((8, PIECES, 128), jnp.bfloat16)

    @pl.loop(0, TOKENS)
    def place(token):
        row = rows[pl.ds(pl.multiple_of(token * PIECES, PIECES), PIECES), :].astype(jnp.bfloat16)
        for choice in range(TOP):
            outgoing[slots[token, choice]] = row


def expert_kernel(incoming, w_gate, w_up, w_down, out, gate_buf, up_buf, down_buf, sems, wide, rows):
    def fetch(source, target, index):
        copy = pltpu.make_async_copy(source, target, sems.at[index])
        copy.start()
        return copy

    gates, ups, downs = [], [], []
    for part in range(3):
        columns = pl.ds(part * 256, 256)
        gates.append(fetch(w_gate.at[0, :, columns], gate_buf.at[part], part))
        ups.append(fetch(w_up.at[0, :, columns], up_buf.at[part], 3 + part))
    for part in range(4):
        columns = pl.ds(part * 1024, 1024)
        downs.append(fetch(w_down.at[0, :, columns], down_buf.at[part], 6 + part))

    @pl.loop(0, SLOTS // 32)
    def widen(group):
        wide[pl.ds(group * 32 * PIECES, 32 * PIECES), :] = incoming[
            pl.ds(group * 32 * PIECES, 32 * PIECES), :
        ].astype(jnp.float32)

    for piece in range(PIECES):
        rows[:, piece * 128 : (piece + 1) * 128] = wide[
            pl.ds(piece, SLOTS, stride=PIECES), :
        ].astype(jnp.bfloat16)
    actives = []
    for part in range(3):
        gates[part].wait()
        gate = jnp.dot(rows[...], gate_buf[part], preferred_element_type=jnp.float32)
        ups[part].wait()
        upward = jnp.dot(rows[...], up_buf[part], preferred_element_type=jnp.float32)
        actives.append((gate / (1.0 + jnp.exp(-gate)) * upward).astype(jnp.bfloat16))
    active = jnp.concatenate(actives, axis=1)
    for part in range(4):
        downs[part].wait()
        for half in range(2):
            produced = jnp.dot(
                active,
                down_buf[part, :, half * 512 : (half + 1) * 512],
                preferred_element_type=jnp.float32,
            )
            for lane in range(4):
                piece = part * 8 + half * 4 + lane
                wide[pl.ds(piece, SLOTS, stride=PIECES), :] = produced[
                    :, lane * 128 : (lane + 1) * 128
                ]

    @pl.loop(0, SLOTS // 32)
    def narrow(group):
        out[pl.ds(group * 32 * PIECES, 32 * PIECES), :] = wide[
            pl.ds(group * 32 * PIECES, 32 * PIECES), :
        ].astype(jnp.bfloat16)


def mix_kernel(slots, weights, returned, out, rows):
    @pl.loop(0, TOKENS)
    def gather(token):
        total = jnp.zeros((PIECES, 128), jnp.float32)
        for choice in range(TOP):
            total = total + weights[token, choice] * returned[slots[token, choice]].astype(
                jnp.float32
            )
        rows[pl.ds(pl.multiple_of(token * PIECES, PIECES), PIECES), :] = total

    for piece in range(PIECES):
        out[:, piece * 128 : (piece + 1) * 128] = rows[pl.ds(piece, TOKENS, stride=PIECES), :]


def swap_cores(array):
    return lax.ppermute(array, "c", [(0, 1), (1, 0)])


def gather_blocks(block):
    spread = jnp.broadcast_to(block[None], (8,) + block.shape)
    return lax.all_to_all(spread, CTX, split_axis=0, concat_axis=0, tiled=True)


def on_device(
    queries,
    keys,
    values,
    out_proj,
    residual,
    norm_gain,
    routes,
    route_weights,
    w_gate,
    w_up,
    w_down,
):
    ctx_index = lax.axis_index(CTX)
    core = lax.axis_index("c")
    shared_head = lax.axis_index(CHIPS) // 2
    own_keys = lax.dynamic_slice_in_dim(keys, shared_head * HEAD_WIDTH, HEAD_WIDTH, 1)
    own_values = lax.dynamic_slice_in_dim(values, shared_head * HEAD_WIDTH, HEAD_WIDTH, 1)
    blocks = gather_blocks(jnp.concatenate([own_keys, own_values], axis=1))
    split = queries.reshape(8, 2, TOKENS, 256)
    own_queries = lax.dynamic_index_in_dim(split, core, 1, False).reshape(128, 256)
    sent_queries = lax.dynamic_index_in_dim(split, 1 - core, 1, False).reshape(128, 256)
    twin_queries = swap_cores(sent_queries)
    twin_proj = swap_cores(out_proj)

    slots = pl.pallas_call(
        slots_kernel,
        out_shape=jax.ShapeDtypeStruct((TOKENS, TOP), jnp.int32),
        in_specs=[SMEM],
        out_specs=SMEM,
        scratch_shapes=[pltpu.SMEM((EXPERTS,), jnp.int32)],
        name="number_slots",
    )(routes)

    place = jnp.stack([ctx_index, core]).astype(jnp.int32)
    partial = pl.pallas_call(
        attention_kernel,
        out_shape=jax.ShapeDtypeStruct((128, D), jnp.bfloat16),
        in_specs=[SMEM, VMEM, VMEM, VMEM, HBM, HBM],
        out_specs=VMEM,
        scratch_shapes=[
            pltpu.VMEM((512, D), jnp.bfloat16),
            pltpu.SemaphoreType.DMA((2,)),
            pltpu.VMEM((512, 128), jnp.float32),
            pltpu.VMEM((512, 128), jnp.float32),
            pltpu.VMEM((512, 128), jnp.float32),
        ],
        compiler_params=pltpu.CompilerParams(vmem_limit_bytes=24 * MIB),
        name="attend_project",
    )(place, own_queries, twin_queries, blocks, out_proj, twin_proj)

    shares = lax.all_to_all(
        partial.reshape(8, TOKENS, D), CHIPS, split_axis=0, concat_axis=0, tiled=True
    )
    hidden_state, outgoing = pl.pallas_call(
        norm_kernel,
        out_shape=(
            jax.ShapeDtypeStruct((TOKENS, D), jnp.bfloat16),
            jax.ShapeDtypeStruct((SLOTS, PIECES, 128), jnp.bfloat16),
        ),
        in_specs=[SMEM, VMEM, VMEM, VMEM],
        out_specs=(VMEM, VMEM),
        scratch_shapes=[pltpu.VMEM((TOKENS * PIECES, 128), jnp.float32)],
        compiler_params=pltpu.CompilerParams(vmem_limit_bytes=16 * MIB),
        name="norm_dispatch",
    )(slots, shares, residual, norm_gain.reshape(1, D))

    incoming = lax.all_to_all(
        outgoing.reshape(EXPERTS, CAP * PIECES, 128), ALL, split_axis=0, concat_axis=0, tiled=True
    )
    produced = pl.pallas_call(
        expert_kernel,
        out_shape=jax.ShapeDtypeStruct((SLOTS * PIECES, 128), jnp.bfloat16),
        in_specs=[VMEM, HBM, HBM, HBM],
        out_specs=VMEM,
        scratch_shapes=[
            pltpu.VMEM((3, D, 256), jnp.bfloat16),
            pltpu.VMEM((3, D, 256), jnp.bfloat16),
            pltpu.VMEM((4, FF, 1024), jnp.bfloat16),
            pltpu.SemaphoreType.DMA((10,)),
            pltpu.VMEM((SLOTS * PIECES, 128), jnp.float32),
            pltpu.VMEM((SLOTS, D), jnp.bfloat16),
        ],
        compiler_params=pltpu.CompilerParams(vmem_limit_bytes=48 * MIB),
        name="expert_rows",
    )(incoming.reshape(SLOTS * PIECES, 128), w_gate, w_up, w_down)
    returned = lax.all_to_all(
        produced.reshape(EXPERTS, CAP * PIECES, 128), ALL, split_axis=0, concat_axis=0, tiled=True
    )
    expert_mix = pl.pallas_call(
        mix_kernel,
        out_shape=jax.ShapeDtypeStruct((TOKENS, D), jnp.float32),
        in_specs=[SMEM, SMEM, VMEM],
        out_specs=VMEM,
        scratch_shapes=[pltpu.VMEM((TOKENS * PIECES, 128), jnp.float32)],
        compiler_params=pltpu.CompilerParams(vmem_limit_bytes=16 * MIB),
        name="mix",
    )(slots, route_weights, returned.reshape(SLOTS, PIECES, 128))
    return (hidden_state, expert_mix)


def solution(mesh):
    fine = Mesh(mesh.devices.reshape(4, 2, 2, 4, 2), ALL)
    exp = ("yh", "z", "c")
    placed = (
        P(CTX, exp),
        P(CTX, None),
        P(CTX, None),
        P(exp, None),
        P(ALL, None),
        P(),
        P(ALL, None),
        P(ALL, None),
        P(ALL, None, None),
        P(ALL, None, None),
        P(ALL, None, None),
    )
    return jax.shard_map(
        on_device,
        mesh=fine,
        in_specs=placed,
        out_specs=(P(ALL, None), P(ALL, None)),
        check_vma=False,
    )
```

```python
import math

import jax
import jax.numpy as jnp
from jax import lax
from jax.experimental import pallas as pl
from jax.experimental.pallas import tpu as pltpu
from jax.sharding import Mesh
from jax.sharding import PartitionSpec as P

D = 4096
HEAD_WIDTH = 128
TOP = 8
TOKENS = 16
EXPERTS = 128
CAP = 2
SLOTS = EXPERTS * CAP
BLOCK = 256
FF = 768
PIECES = D // 128
CTX = ("x", "yl")
CHIPS = ("yh", "z")
ALL = ("x", "yl", "yh", "z", "c")
INV_ROOT = 1.0 / math.sqrt(HEAD_WIDTH)
MIB = 1 << 20

VMEM = pl.BlockSpec(memory_space=pltpu.VMEM)
SMEM = pl.BlockSpec(memory_space=pltpu.SMEM)
HBM = pl.BlockSpec(memory_space=pltpu.HBM)


def attention_kernel(place, own_queries, twin_queries, *refs):
    arrived, (own_proj, twin_proj, out, w_buf, sems, raw, tops, sums, acc, blocks) = refs[:8], refs[8:]
    copies = [
        pltpu.make_async_copy(own_proj, w_buf.at[pl.ds(0, 256)], sems.at[0]),
        pltpu.make_async_copy(twin_proj, w_buf.at[pl.ds(256, 256)], sems.at[1]),
    ]
    for copy in copies:
        copy.start()
    own_block = place[0]
    core = place[1]
    for index, block in enumerate(arrived):
        blocks[place[2 + index]] = block[...]
    stacked = jnp.concatenate(
        [
            own_queries[:, 0:128],
            own_queries[:, 128:256],
            twin_queries[:, 0:128],
            twin_queries[:, 128:256],
        ],
        axis=0,
    )

    def products(block):
        return lax.dot_general(
            stacked,
            blocks[block, :, 0:128],
            (((1,), (1,)), ((), ())),
            preferred_element_type=jnp.float32,
        )

    def columns_of(block):
        return pl.ds(pl.multiple_of(block * BLOCK, BLOCK), BLOCK)

    row = lax.broadcasted_iota(jnp.int32, (512, BLOCK), 0) % 128
    position = (row // TOKENS) * (2 * TOKENS) + core * TOKENS + row % TOKENS
    visible = lax.broadcasted_iota(jnp.int32, (512, BLOCK), 1) <= position
    latest = jnp.where(visible, products(own_block), -1e30)
    raw[:, columns_of(own_block)] = latest
    tops[...] = jnp.maximum(latest[:, 0:128], latest[:, 128:256])

    @pl.loop(0, own_block)
    def score(block):
        earlier = products(block)
        raw[:, columns_of(block)] = earlier
        tops[...] = jnp.maximum(
            tops[...], jnp.maximum(earlier[:, 0:128], earlier[:, 128:256])
        )

    tops[...] = jnp.broadcast_to(jnp.max(tops[...], axis=1, keepdims=True), (512, 128))
    sums[...] = jnp.zeros((512, 128), jnp.float32)
    acc[...] = jnp.zeros((512, 128), jnp.float32)

    @pl.loop(0, own_block + 1)
    def weigh(block):
        top = tops[...]
        scores = raw[:, columns_of(block)]
        left = jnp.exp((scores[:, 0:128] - top) * INV_ROOT)
        right = jnp.exp((scores[:, 128:256] - top) * INV_ROOT)
        sums[...] += left + right
        probs = jnp.concatenate([left.astype(jnp.bfloat16), right.astype(jnp.bfloat16)], axis=1)
        acc[...] += jnp.dot(
            probs, blocks[block, :, 128:256], preferred_element_type=jnp.float32
        )

    total = jnp.sum(sums[...], axis=1, keepdims=True)
    attended = (acc[...] / total).astype(jnp.bfloat16)
    wide = jnp.concatenate([attended[h * 128 : (h + 1) * 128] for h in range(4)], axis=1)
    for copy in copies:
        copy.wait()

    for piece in range(D // 512):
        columns = slice(piece * 512, (piece + 1) * 512)
        out[:, columns] = jnp.dot(
            wide, w_buf[:, columns], preferred_element_type=jnp.float32
        ).astype(jnp.bfloat16)


def slots_kernel(routes, slots, counts):
    @pl.loop(0, EXPERTS)
    def clear(expert):
        counts[expert] = 0

    @pl.loop(0, TOKENS)
    def number(token):
        for choice in range(TOP):
            expert = routes[token, choice]
            rank = counts[expert]
            counts[expert] = rank + 1
            slots[token, choice] = expert * CAP + rank


def norm_kernel(listed, shares, residual, gain, hidden, outgoing, rows, slots, sem):
    listing = pltpu.make_async_copy(listed, slots, sem)
    listing.start()
    total = residual[...].astype(jnp.float32)
    for share in range(8):
        total = total + shares[share].astype(jnp.float32)
    state = total.astype(jnp.bfloat16)
    hidden[...] = state
    wide = state.astype(jnp.float32)
    scale = lax.rsqrt(jnp.mean(wide * wide, axis=1, keepdims=True) + 1e-6)
    normed = wide * scale * gain[...]
    for piece in range(PIECES):
        rows[pl.ds(piece, TOKENS, stride=PIECES), :] = normed[:, piece * 128 : (piece + 1) * 128]

    @pl.loop(0, SLOTS // 8)
    def clear(group):
        outgoing[pl.ds(group * 8, 8)] = jnp.zeros((8, PIECES, 128), jnp.bfloat16)

    listing.wait()

    @pl.loop(0, TOKENS)
    def place(token):
        row = rows[pl.ds(pl.multiple_of(token * PIECES, PIECES), PIECES), :].astype(jnp.bfloat16)
        for choice in range(TOP):
            outgoing[slots[token, choice]] = row


def expert_kernel(
    incoming,
    w_gate,
    w_up,
    w_down,
    out,
    gate_buf,
    up_buf,
    down_buf,
    fetch_sems,
    gate,
    upward,
    wide,
    rows,
    stage,
    sems,
):
    def pair(part):
        span = pl.ds(part * 1024, 1024)
        return [
            pltpu.make_async_copy(
                w_gate.at[0, span], gate_buf.at[span], fetch_sems.at[2 * part]
            ),
            pltpu.make_async_copy(
                w_up.at[0, span], up_buf.at[span], fetch_sems.at[2 * part + 1]
            ),
        ]

    def down(part):
        return pltpu.make_async_copy(
            w_down.at[0, :, pl.ds(part * 1024, 1024)], down_buf.at[part], fetch_sems.at[8 + part]
        )

    pairs = [pair(part) for part in range(4)]
    downs = [down(part) for part in range(4)]
    then = [pairs[2], pairs[3], downs[0:2], downs[2:4]]
    for copy in pairs[0] + pairs[1]:
        copy.start()

    @pl.loop(0, SLOTS // 32)
    def widen(group):
        wide[pl.ds(group * 32 * PIECES, 32 * PIECES), :] = incoming[
            pl.ds(group * 32 * PIECES, 32 * PIECES), :
        ].astype(jnp.float32)

    for part in range(4):
        for piece in range(part * 8, part * 8 + 8):
            rows[:, piece * 128 : (piece + 1) * 128] = wide[
                pl.ds(piece, SLOTS, stride=PIECES), :
            ].astype(jnp.bfloat16)
        span = slice(part * 1024, (part + 1) * 1024)
        for copy in pairs[part]:
            copy.wait()
        for copy in then[part]:
            copy.start()
        for total, weights in ((gate, gate_buf), (upward, up_buf)):
            product = jnp.dot(rows[:, span], weights[span, :], preferred_element_type=jnp.float32)
            if part:
                total[...] += product
            else:
                total[...] = product
    active = (gate[...] / (1.0 + jnp.exp(-gate[...])) * upward[...]).astype(jnp.bfloat16)
    for part in range(8):
        if part % 2 == 0:
            downs[part // 2].wait()
        half = part % 2
        produced = jnp.dot(
            active,
            down_buf[part // 2, :, half * 512 : (half + 1) * 512],
            preferred_element_type=jnp.float32,
        )
        for lane in range(4):
            piece = part * 4 + lane
            for tile in range(SLOTS // 8):
                start = tile * 8 * PIECES + piece * 8
                wide[start : start + 8, :] = produced[
                    tile * 8 : (tile + 1) * 8, lane * 128 : (lane + 1) * 128
                ]
    copies = []
    for quarter in range(4):

        @pl.loop(quarter * 8, quarter * 8 + 8)
        def narrow(tile):
            for row in range(8):
                start = pl.multiple_of((tile * 8 + row) * PIECES, PIECES)
                stage[pl.ds(start, PIECES), :] = wide[
                    pl.ds(tile * 8 * PIECES + row, PIECES, stride=8), :
                ].astype(jnp.bfloat16)

        span = pl.ds(quarter * 64 * PIECES, 64 * PIECES)
        copy = pltpu.make_async_copy(stage.at[span], out.at[span], sems.at[quarter])
        copy.start()
        copies.append(copy)
    for copy in copies:
        copy.wait()


def mix_kernel(slots, weights, returned, out, rows):
    @pl.loop(0, TOKENS)
    def gather(token):
        total = jnp.zeros((PIECES, 128), jnp.float32)
        for choice in range(TOP):
            total = total + weights[token, choice] * returned[slots[token, choice]].astype(
                jnp.float32
            )
        rows[pl.ds(pl.multiple_of(token * PIECES, PIECES), PIECES), :] = total

    for piece in range(PIECES):
        out[:, piece * 128 : (piece + 1) * 128] = rows[pl.ds(piece, TOKENS, stride=PIECES), :]


def swap_cores(array):
    return lax.ppermute(array, "c", [(0, 1), (1, 0)])


def gather_blocks(block):
    fetched, handed = [], []
    for step in range(4):
        pairs = []
        for x in range(4):
            for y in range(2):
                for core in range(2):
                    target_x = (x + step) % 4
                    target_y = y if core == y else 1 - y
                    pairs.append(((x * 2 + y) * 2 + core, (target_x * 2 + target_y) * 2 + y))
        fetched.append(lax.ppermute(block, ("x", "yl", "c"), pairs))
        handed.append(swap_cores(fetched[-1]))
    x, core = lax.axis_index("x"), lax.axis_index("c")
    rings = [lax.rem(x - step + 4, 4) * 2 for step in range(4)]
    origins = [ring + core for ring in rings] + [ring + 1 - core for ring in rings]
    return fetched + handed, origins


def on_device(
    queries,
    keys,
    values,
    out_proj,
    residual,
    norm_gain,
    routes,
    route_weights,
    w_gate,
    w_up,
    w_down,
):
    ctx_index = lax.axis_index(CTX)
    core = lax.axis_index("c")
    shared_head = lax.axis_index(CHIPS) // 2
    own_keys = lax.dynamic_slice_in_dim(keys, shared_head * HEAD_WIDTH, HEAD_WIDTH, 1)
    own_values = lax.dynamic_slice_in_dim(values, shared_head * HEAD_WIDTH, HEAD_WIDTH, 1)
    blocks, origins = gather_blocks(jnp.concatenate([own_keys, own_values], axis=1))
    split = queries.reshape(8, 2, TOKENS, 256)
    own_queries = lax.dynamic_index_in_dim(split, core, 1, False).reshape(128, 256)
    sent_queries = lax.dynamic_index_in_dim(split, 1 - core, 1, False).reshape(128, 256)
    twin_queries = swap_cores(sent_queries)
    twin_proj = swap_cores(out_proj)

    slots = pl.pallas_call(
        slots_kernel,
        out_shape=jax.ShapeDtypeStruct((TOKENS, TOP), jnp.int32),
        in_specs=[SMEM],
        out_specs=SMEM,
        scratch_shapes=[pltpu.SMEM((EXPERTS,), jnp.int32)],
        name="number_slots",
    )(routes)

    place = jnp.stack([ctx_index, core] + origins).astype(jnp.int32)
    partial = pl.pallas_call(
        attention_kernel,
        out_shape=jax.ShapeDtypeStruct((128, D), jnp.bfloat16),
        in_specs=[SMEM] + [VMEM] * 10 + [HBM, HBM],
        out_specs=VMEM,
        scratch_shapes=[
            pltpu.VMEM((512, D), jnp.bfloat16),
            pltpu.SemaphoreType.DMA((2,)),
            pltpu.VMEM((512, 8 * BLOCK), jnp.float32),
            pltpu.VMEM((512, 128), jnp.float32),
            pltpu.VMEM((512, 128), jnp.float32),
            pltpu.VMEM((512, 128), jnp.float32),
            pltpu.VMEM((8, BLOCK, 256), jnp.bfloat16),
        ],
        compiler_params=pltpu.CompilerParams(vmem_limit_bytes=24 * MIB),
        name="attend_project",
    )(place, own_queries, twin_queries, *blocks, out_proj, twin_proj)

    shares = lax.all_to_all(
        partial.reshape(8, TOKENS, D), CHIPS, split_axis=0, concat_axis=0, tiled=True
    )
    hidden_state, outgoing = pl.pallas_call(
        norm_kernel,
        out_shape=(
            jax.ShapeDtypeStruct((TOKENS, D), jnp.bfloat16),
            jax.ShapeDtypeStruct((SLOTS, PIECES, 128), jnp.bfloat16),
        ),
        in_specs=[HBM, VMEM, VMEM, VMEM],
        out_specs=(VMEM, VMEM),
        scratch_shapes=[
            pltpu.VMEM((TOKENS * PIECES, 128), jnp.float32),
            pltpu.SMEM((TOKENS, TOP), jnp.int32),
            pltpu.SemaphoreType.DMA,
        ],
        compiler_params=pltpu.CompilerParams(vmem_limit_bytes=16 * MIB),
        name="norm_dispatch",
    )(slots, shares, residual, norm_gain.reshape(1, D))

    incoming = lax.all_to_all(
        outgoing.reshape(EXPERTS, CAP * PIECES, 128), ALL, split_axis=0, concat_axis=0, tiled=True
    )
    produced = pl.pallas_call(
        expert_kernel,
        out_shape=pltpu.HBM((SLOTS * PIECES, 128), jnp.bfloat16),
        in_specs=[VMEM, HBM, HBM, HBM],
        out_specs=HBM,
        scratch_shapes=[
            pltpu.VMEM((D, FF), jnp.bfloat16),
            pltpu.VMEM((D, FF), jnp.bfloat16),
            pltpu.VMEM((4, FF, 1024), jnp.bfloat16),
            pltpu.SemaphoreType.DMA((12,)),
            pltpu.VMEM((SLOTS, FF), jnp.float32),
            pltpu.VMEM((SLOTS, FF), jnp.float32),
            pltpu.VMEM((SLOTS * PIECES, 128), jnp.float32),
            pltpu.VMEM((SLOTS, D), jnp.bfloat16),
            pltpu.VMEM((SLOTS * PIECES, 128), jnp.bfloat16),
            pltpu.SemaphoreType.DMA((4,)),
        ],
        compiler_params=pltpu.CompilerParams(vmem_limit_bytes=56 * MIB),
        name="expert_rows",
    )(incoming.reshape(SLOTS * PIECES, 128), w_gate, w_up, w_down)
    returned = lax.all_to_all(
        produced.reshape(EXPERTS, CAP * PIECES, 128), ALL, split_axis=0, concat_axis=0, tiled=True
    )
    expert_mix = pl.pallas_call(
        mix_kernel,
        out_shape=jax.ShapeDtypeStruct((TOKENS, D), jnp.float32),
        in_specs=[SMEM, SMEM, VMEM],
        out_specs=VMEM,
        scratch_shapes=[pltpu.VMEM((TOKENS * PIECES, 128), jnp.float32)],
        compiler_params=pltpu.CompilerParams(vmem_limit_bytes=16 * MIB),
        name="mix",
    )(slots, route_weights, returned.reshape(SLOTS, PIECES, 128))
    return (hidden_state, expert_mix)


def solution(mesh):
    fine = Mesh(mesh.devices.reshape(4, 2, 2, 4, 2), ALL)
    exp = ("yh", "z", "c")
    placed = (
        P(CTX, exp),
        P(CTX, None),
        P(CTX, None),
        P(exp, None),
        P(ALL, None),
        P(),
        P(ALL, None),
        P(ALL, None),
        P(ALL, None, None),
        P(ALL, None, None),
        P(ALL, None, None),
    )
    return jax.shard_map(
        on_device,
        mesh=fine,
        in_specs=placed,
        out_specs=(P(ALL, None), P(ALL, None)),
        check_vma=False,
    )
```

```python
import math

import jax
import jax.numpy as jnp
from jax import lax
from jax.experimental import pallas as pl
from jax.experimental.pallas import tpu as pltpu
from jax.sharding import Mesh
from jax.sharding import PartitionSpec as P

D = 4096
HEAD_WIDTH = 128
TOP = 8
TOKENS = 16
EXPERTS = 128
CAP = 2
SLOTS = EXPERTS * CAP
BLOCK = 256
FF = 768
PIECES = D // 128
CTX = ("x", "yl")
CHIPS = ("yh", "z")
ALL = ("x", "yl", "yh", "z", "c")
INV_ROOT = 1.0 / math.sqrt(HEAD_WIDTH)
MIB = 1 << 20

VMEM = pl.BlockSpec(memory_space=pltpu.VMEM)
SMEM = pl.BlockSpec(memory_space=pltpu.SMEM)
HBM = pl.BlockSpec(memory_space=pl.ANY)


def attention_kernel(place, own_queries, twin_queries, *refs):
    arrived, (own_proj, twin_proj, out, w_buf, sems, raw, tops, sums, acc, blocks) = refs[:8], refs[8:]
    copies = [
        pltpu.make_async_copy(own_proj, w_buf.at[pl.ds(0, 256)], sems.at[0]),
        pltpu.make_async_copy(twin_proj, w_buf.at[pl.ds(256, 256)], sems.at[1]),
    ]
    for copy in copies:
        copy.start()
    own_block = place[0]
    core = place[1]
    for index, block in enumerate(arrived):
        blocks[place[2 + index]] = block[...]
    stacked = jnp.concatenate(
        [
            own_queries[:, 0:128],
            own_queries[:, 128:256],
            twin_queries[:, 0:128],
            twin_queries[:, 128:256],
        ],
        axis=0,
    )

    def products(block):
        return lax.dot_general(
            stacked,
            blocks[block, :, 0:128],
            (((1,), (1,)), ((), ())),
            preferred_element_type=jnp.float32,
        )

    def columns_of(block):
        return pl.ds(pl.multiple_of(block * BLOCK, BLOCK), BLOCK)

    row = lax.broadcasted_iota(jnp.int32, (512, BLOCK), 0) % 128
    position = (row // TOKENS) * (2 * TOKENS) + core * TOKENS + row % TOKENS
    visible = lax.broadcasted_iota(jnp.int32, (512, BLOCK), 1) <= position
    latest = jnp.where(visible, products(own_block), -1e30)
    raw[:, columns_of(own_block)] = latest
    tops[...] = jnp.maximum(latest[:, 0:128], latest[:, 128:256])

    @pl.loop(0, own_block)
    def score(block):
        earlier = products(block)
        raw[:, columns_of(block)] = earlier
        tops[...] = jnp.maximum(
            tops[...], jnp.maximum(earlier[:, 0:128], earlier[:, 128:256])
        )

    tops[...] = jnp.broadcast_to(jnp.max(tops[...], axis=1, keepdims=True), (512, 128))
    sums[...] = jnp.zeros((512, 128), jnp.float32)
    acc[...] = jnp.zeros((512, 128), jnp.float32)

    @pl.loop(0, own_block + 1)
    def weigh(block):
        top = tops[...]
        scores = raw[:, columns_of(block)]
        left = jnp.exp((scores[:, 0:128] - top) * INV_ROOT)
        right = jnp.exp((scores[:, 128:256] - top) * INV_ROOT)
        sums[...] += left + right
        probs = jnp.concatenate([left.astype(jnp.bfloat16), right.astype(jnp.bfloat16)], axis=1)
        acc[...] += jnp.dot(
            probs, blocks[block, :, 128:256], preferred_element_type=jnp.float32
        )

    total = jnp.sum(sums[...], axis=1, keepdims=True)
    attended = (acc[...] / total).astype(jnp.bfloat16)
    wide = jnp.concatenate([attended[h * 128 : (h + 1) * 128] for h in range(4)], axis=1)
    for copy in copies:
        copy.wait()

    for piece in range(D // 512):
        columns = slice(piece * 512, (piece + 1) * 512)
        out[:, columns] = jnp.dot(
            wide, w_buf[:, columns], preferred_element_type=jnp.float32
        ).astype(jnp.bfloat16)


def slots_kernel(routes, weights, listed, weighed, slots, held, counts, sems):
    @pl.loop(0, EXPERTS)
    def clear(expert):
        counts[expert] = 0

    @pl.loop(0, TOKENS)
    def number(token):
        for choice in range(TOP):
            expert = routes[token, choice]
            rank = counts[expert]
            counts[expert] = rank + 1
            slots[token, choice] = expert * CAP + rank
            held[token, choice] = weights[token, choice]

    copies = [
        pltpu.make_async_copy(slots, listed, sems.at[0]),
        pltpu.make_async_copy(held, weighed, sems.at[1]),
    ]
    for copy in copies:
        copy.start()
    for copy in copies:
        copy.wait()


def norm_kernel(listed, shares, residual, gain, hidden, outgoing, rows, slots, sem):
    listing = pltpu.make_async_copy(listed, slots, sem)
    listing.start()
    total = residual[...].astype(jnp.float32)
    for share in range(8):
        total = total + shares[share].astype(jnp.float32)
    state = total.astype(jnp.bfloat16)
    hidden[...] = state
    wide = state.astype(jnp.float32)
    scale = lax.rsqrt(jnp.mean(wide * wide, axis=1, keepdims=True) + 1e-6)
    normed = wide * scale * gain[...]
    for piece in range(PIECES):
        rows[pl.ds(piece, TOKENS, stride=PIECES), :] = normed[:, piece * 128 : (piece + 1) * 128]

    @pl.loop(0, SLOTS // 8)
    def clear(group):
        outgoing[pl.ds(group * 8, 8)] = jnp.zeros((8, PIECES, 128), jnp.bfloat16)

    listing.wait()

    @pl.loop(0, TOKENS)
    def place(token):
        row = rows[pl.ds(pl.multiple_of(token * PIECES, PIECES), PIECES), :].astype(jnp.bfloat16)
        for choice in range(TOP):
            outgoing[slots[token, choice]] = row


def expert_kernel(
    incoming,
    w_gate,
    w_up,
    w_down,
    out,
    gate_buf,
    up_buf,
    down_buf,
    fetch_sems,
    gate,
    upward,
    wide,
    rows,
    stage,
    sems,
):
    def pair(part):
        span = pl.ds(part * 1024, 1024)
        return [
            pltpu.make_async_copy(
                w_gate.at[0, span], gate_buf.at[span], fetch_sems.at[2 * part]
            ),
            pltpu.make_async_copy(
                w_up.at[0, span], up_buf.at[span], fetch_sems.at[2 * part + 1]
            ),
        ]

    def down(part):
        return pltpu.make_async_copy(
            w_down.at[0, :, pl.ds(part * 1024, 1024)], down_buf.at[part], fetch_sems.at[8 + part]
        )

    pairs = [pair(part) for part in range(4)]
    downs = [down(part) for part in range(4)]
    for copy in pairs[0] + pairs[1] + pairs[2] + pairs[3] + downs:
        copy.start()

    @pl.loop(0, SLOTS // 32)
    def widen(group):
        wide[pl.ds(group * 32 * PIECES, 32 * PIECES), :] = incoming[
            pl.ds(group * 32 * PIECES, 32 * PIECES), :
        ].astype(jnp.float32)

    for piece in range(PIECES):
        rows[:, piece * 128 : (piece + 1) * 128] = wide[
            pl.ds(piece, SLOTS, stride=PIECES), :
        ].astype(jnp.bfloat16)
    for part in range(4):
        span = slice(part * 1024, (part + 1) * 1024)
        for copy in pairs[part]:
            copy.wait()
        for total, weights in ((gate, gate_buf), (upward, up_buf)):
            product = jnp.dot(rows[:, span], weights[span, :], preferred_element_type=jnp.float32)
            if part:
                total[...] += product
            else:
                total[...] = product
    active = (gate[...] / (1.0 + jnp.exp(-gate[...])) * upward[...]).astype(jnp.bfloat16)
    for part in range(8):
        if part % 2 == 0:
            downs[part // 2].wait()
        half = part % 2
        produced = jnp.dot(
            active,
            down_buf[part // 2, :, half * 512 : (half + 1) * 512],
            preferred_element_type=jnp.float32,
        )
        for lane in range(4):
            piece = part * 4 + lane
            for tile in range(SLOTS // 8):
                start = tile * 8 * PIECES + piece * 8
                wide[start : start + 8, :] = produced[
                    tile * 8 : (tile + 1) * 8, lane * 128 : (lane + 1) * 128
                ]
    copies = []
    for quarter in range(4):

        @pl.loop(quarter * 8, quarter * 8 + 8)
        def narrow(tile):
            for row in range(8):
                start = pl.multiple_of((tile * 8 + row) * PIECES, PIECES)
                stage[pl.ds(start, PIECES), :] = wide[
                    pl.ds(tile * 8 * PIECES + row, PIECES, stride=8), :
                ].astype(jnp.bfloat16)

        span = pl.ds(quarter * 64 * PIECES, 64 * PIECES)
        copy = pltpu.make_async_copy(stage.at[span], out.at[span], sems.at[quarter])
        copy.start()
        copies.append(copy)
    for copy in copies:
        copy.wait()


def mix_kernel(slots, weights, returned, out, rows):
    @pl.loop(0, TOKENS)
    def gather(token):
        total = jnp.zeros((PIECES, 128), jnp.float32)
        for choice in range(TOP):
            total = total + weights[token, choice] * returned[slots[token, choice]].astype(
                jnp.float32
            )
        rows[pl.ds(pl.multiple_of(token * PIECES, PIECES), PIECES), :] = total

    for piece in range(PIECES):
        out[:, piece * 128 : (piece + 1) * 128] = rows[pl.ds(piece, TOKENS, stride=PIECES), :]


def swap_cores(array):
    return lax.ppermute(array, "c", [(0, 1), (1, 0)])


def gather_blocks(block):
    fetched, handed = [], []
    for step in range(4):
        pairs = []
        for x in range(4):
            for y in range(2):
                for core in range(2):
                    target_x = (x + step) % 4
                    target_y = y if core == y else 1 - y
                    pairs.append(((x * 2 + y) * 2 + core, (target_x * 2 + target_y) * 2 + y))
        fetched.append(lax.ppermute(block, ("x", "yl", "c"), pairs))
        handed.append(swap_cores(fetched[-1]))
    x, core = lax.axis_index("x"), lax.axis_index("c")
    rings = [lax.rem(x - step + 4, 4) * 2 for step in range(4)]
    origins = [ring + core for ring in rings] + [ring + 1 - core for ring in rings]
    return fetched + handed, origins


def on_device(
    queries,
    keys,
    values,
    out_proj,
    residual,
    norm_gain,
    routes,
    route_weights,
    w_gate,
    w_up,
    w_down,
):
    ctx_index = lax.axis_index(CTX)
    core = lax.axis_index("c")
    shared_head = lax.axis_index(CHIPS) // 2
    own_keys = lax.dynamic_slice_in_dim(keys, shared_head * HEAD_WIDTH, HEAD_WIDTH, 1)
    own_values = lax.dynamic_slice_in_dim(values, shared_head * HEAD_WIDTH, HEAD_WIDTH, 1)
    blocks, origins = gather_blocks(jnp.concatenate([own_keys, own_values], axis=1))
    split = queries.reshape(8, 2, TOKENS, 256)
    own_queries = lax.dynamic_index_in_dim(split, core, 1, False).reshape(128, 256)
    sent_queries = lax.dynamic_index_in_dim(split, 1 - core, 1, False).reshape(128, 256)
    twin_queries = swap_cores(sent_queries)
    twin_proj = swap_cores(out_proj)

    slots, weights = pl.pallas_call(
        slots_kernel,
        out_shape=(
            jax.ShapeDtypeStruct((TOKENS, TOP), jnp.int32),
            jax.ShapeDtypeStruct((TOKENS, TOP), jnp.float32),
        ),
        in_specs=[SMEM, SMEM],
        out_specs=(HBM, HBM),
        scratch_shapes=[
            pltpu.SMEM((TOKENS, TOP), jnp.int32),
            pltpu.SMEM((TOKENS, TOP), jnp.float32),
            pltpu.SMEM((EXPERTS,), jnp.int32),
            pltpu.SemaphoreType.DMA((2,)),
        ],
        name="number_slots",
    )(routes, route_weights)

    place = jnp.stack([ctx_index, core] + origins).astype(jnp.int32)
    partial = pl.pallas_call(
        attention_kernel,
        out_shape=jax.ShapeDtypeStruct((128, D), jnp.bfloat16),
        in_specs=[SMEM] + [VMEM] * 10 + [HBM, HBM],
        out_specs=VMEM,
        scratch_shapes=[
            pltpu.VMEM((512, D), jnp.bfloat16),
            pltpu.SemaphoreType.DMA((2,)),
            pltpu.VMEM((512, 8 * BLOCK), jnp.float32),
            pltpu.VMEM((512, 128), jnp.float32),
            pltpu.VMEM((512, 128), jnp.float32),
            pltpu.VMEM((512, 128), jnp.float32),
            pltpu.VMEM((8, BLOCK, 256), jnp.bfloat16),
        ],
        compiler_params=pltpu.CompilerParams(vmem_limit_bytes=24 * MIB),
        name="attend_project",
    )(place, own_queries, twin_queries, *blocks, out_proj, twin_proj)

    shares = lax.all_to_all(
        partial.reshape(8, TOKENS, D), CHIPS, split_axis=0, concat_axis=0, tiled=True
    )
    hidden_state, outgoing = pl.pallas_call(
        norm_kernel,
        out_shape=(
            jax.ShapeDtypeStruct((TOKENS, D), jnp.bfloat16),
            jax.ShapeDtypeStruct((SLOTS, PIECES, 128), jnp.bfloat16),
        ),
        in_specs=[HBM, VMEM, VMEM, VMEM],
        out_specs=(VMEM, VMEM),
        scratch_shapes=[
            pltpu.VMEM((TOKENS * PIECES, 128), jnp.float32),
            pltpu.SMEM((TOKENS, TOP), jnp.int32),
            pltpu.SemaphoreType.DMA,
        ],
        compiler_params=pltpu.CompilerParams(vmem_limit_bytes=16 * MIB),
        name="norm_dispatch",
    )(slots, shares, residual, norm_gain.reshape(1, D))

    incoming = lax.all_to_all(
        outgoing.reshape(EXPERTS, CAP * PIECES, 128), ALL, split_axis=0, concat_axis=0, tiled=True
    )
    produced = pl.pallas_call(
        expert_kernel,
        out_shape=pltpu.HBM((SLOTS * PIECES, 128), jnp.bfloat16),
        in_specs=[VMEM, HBM, HBM, HBM],
        out_specs=HBM,
        scratch_shapes=[
            pltpu.VMEM((D, FF), jnp.bfloat16),
            pltpu.VMEM((D, FF), jnp.bfloat16),
            pltpu.VMEM((4, FF, 1024), jnp.bfloat16),
            pltpu.SemaphoreType.DMA((12,)),
            pltpu.VMEM((SLOTS, FF), jnp.float32),
            pltpu.VMEM((SLOTS, FF), jnp.float32),
            pltpu.VMEM((SLOTS * PIECES, 128), jnp.float32),
            pltpu.VMEM((SLOTS, D), jnp.bfloat16),
            pltpu.VMEM((SLOTS * PIECES, 128), jnp.bfloat16),
            pltpu.SemaphoreType.DMA((4,)),
        ],
        compiler_params=pltpu.CompilerParams(vmem_limit_bytes=56 * MIB),
        name="expert_rows",
    )(incoming.reshape(SLOTS * PIECES, 128), w_gate, w_up, w_down)
    returned = lax.all_to_all(
        produced.reshape(EXPERTS, CAP * PIECES, 128), ALL, split_axis=0, concat_axis=0, tiled=True
    )
    expert_mix = pl.pallas_call(
        mix_kernel,
        out_shape=jax.ShapeDtypeStruct((TOKENS, D), jnp.float32),
        in_specs=[SMEM, SMEM, VMEM],
        out_specs=VMEM,
        scratch_shapes=[pltpu.VMEM((TOKENS * PIECES, 128), jnp.float32)],
        compiler_params=pltpu.CompilerParams(vmem_limit_bytes=16 * MIB),
        name="mix",
    )(slots, weights, returned.reshape(SLOTS, PIECES, 128))
    return (hidden_state, expert_mix)


def solution(mesh):
    fine = Mesh(mesh.devices.reshape(4, 2, 2, 4, 2), ALL)
    exp = ("yh", "z", "c")
    placed = (
        P(CTX, exp),
        P(CTX, None),
        P(CTX, None),
        P(exp, None),
        P(ALL, None),
        P(),
        P(ALL, None),
        P(ALL, None),
        P(ALL, None, None),
        P(ALL, None, None),
        P(ALL, None, None),
    )
    return jax.shard_map(
        on_device,
        mesh=fine,
        in_specs=placed,
        out_specs=(P(ALL, None), P(ALL, None)),
        check_vma=False,
    )
```

```python
import math

import jax
import jax.numpy as jnp
from jax import lax
from jax.experimental import pallas as pl
from jax.experimental.pallas import tpu as pltpu
from jax.sharding import Mesh
from jax.sharding import PartitionSpec as P

D = 4096
HEAD_WIDTH = 128
TOP = 8
TOKENS = 16
EXPERTS = 128
CAP = 2
SLOTS = EXPERTS * CAP
BLOCK = 256
FF = 768
PIECES = D // 128
CTX = ("x", "yl")
CHIPS = ("yh", "z")
ALL = ("x", "yl", "yh", "z", "c")
INV_ROOT = 1.0 / math.sqrt(HEAD_WIDTH)
MIB = 1 << 20

VMEM = pl.BlockSpec(memory_space=pltpu.VMEM)
SMEM = pl.BlockSpec(memory_space=pltpu.SMEM)
HBM = pl.BlockSpec(memory_space=pl.ANY)


def attention_kernel(place, own_queries, twin_queries, *refs):
    arrived, (own_proj, twin_proj, out, w_buf, sems, raw, tops, sums, acc, blocks) = refs[:8], refs[8:]
    copies = [
        pltpu.make_async_copy(own_proj, w_buf.at[pl.ds(0, 256)], sems.at[0]),
        pltpu.make_async_copy(twin_proj, w_buf.at[pl.ds(256, 256)], sems.at[1]),
    ]
    for copy in copies:
        copy.start()
    own_block = place[0]
    core = place[1]
    for index, block in enumerate(arrived):
        blocks[place[2 + index]] = block[...]
    stacked = jnp.concatenate(
        [
            own_queries[:, 0:128],
            own_queries[:, 128:256],
            twin_queries[:, 0:128],
            twin_queries[:, 128:256],
        ],
        axis=0,
    )

    def products(block):
        return lax.dot_general(
            stacked,
            blocks[block, :, 0:128],
            (((1,), (1,)), ((), ())),
            preferred_element_type=jnp.float32,
        )

    def columns_of(block):
        return pl.ds(pl.multiple_of(block * BLOCK, BLOCK), BLOCK)

    row = lax.broadcasted_iota(jnp.int32, (512, BLOCK), 0) % 128
    position = (row // TOKENS) * (2 * TOKENS) + core * TOKENS + row % TOKENS
    visible = lax.broadcasted_iota(jnp.int32, (512, BLOCK), 1) <= position
    latest = jnp.where(visible, products(own_block), -1e30)
    raw[:, columns_of(own_block)] = latest
    tops[...] = jnp.maximum(latest[:, 0:128], latest[:, 128:256])

    @pl.loop(0, own_block)
    def score(block):
        earlier = products(block)
        raw[:, columns_of(block)] = earlier
        tops[...] = jnp.maximum(
            tops[...], jnp.maximum(earlier[:, 0:128], earlier[:, 128:256])
        )

    tops[...] = jnp.broadcast_to(jnp.max(tops[...], axis=1, keepdims=True), (512, 128))
    sums[...] = jnp.zeros((512, 128), jnp.float32)
    acc[...] = jnp.zeros((512, 128), jnp.float32)

    @pl.loop(0, own_block + 1)
    def weigh(block):
        top = tops[...]
        scores = raw[:, columns_of(block)]
        left = jnp.exp((scores[:, 0:128] - top) * INV_ROOT)
        right = jnp.exp((scores[:, 128:256] - top) * INV_ROOT)
        sums[...] += left + right
        probs = jnp.concatenate([left.astype(jnp.bfloat16), right.astype(jnp.bfloat16)], axis=1)
        acc[...] += jnp.dot(
            probs, blocks[block, :, 128:256], preferred_element_type=jnp.float32
        )

    total = jnp.sum(sums[...], axis=1, keepdims=True)
    attended = (acc[...] / total).astype(jnp.bfloat16)
    wide = jnp.concatenate([attended[h * 128 : (h + 1) * 128] for h in range(4)], axis=1)
    for copy in copies:
        copy.wait()

    for piece in range(D // 512):
        columns = slice(piece * 512, (piece + 1) * 512)
        out[:, columns] = jnp.dot(
            wide, w_buf[:, columns], preferred_element_type=jnp.float32
        ).astype(jnp.bfloat16)


def slots_kernel(routes, weights, listed, weighed, slots, held, counts, sems):
    @pl.loop(0, EXPERTS)
    def clear(expert):
        counts[expert] = 0

    @pl.loop(0, TOKENS)
    def number(token):
        for choice in range(TOP):
            expert = routes[token, choice]
            rank = counts[expert]
            counts[expert] = rank + 1
            slots[token, choice] = expert * CAP + rank
            held[token, choice] = weights[token, choice]

    copies = [
        pltpu.make_async_copy(slots, listed, sems.at[0]),
        pltpu.make_async_copy(held, weighed, sems.at[1]),
    ]
    for copy in copies:
        copy.start()
    for copy in copies:
        copy.wait()


def norm_kernel(listed, shares, residual, gain, hidden, outgoing, rows, slots, sem):
    listing = pltpu.make_async_copy(listed, slots, sem)
    listing.start()
    total = residual[...].astype(jnp.float32)
    for share in range(8):
        total = total + shares[share].astype(jnp.float32)
    state = total.astype(jnp.bfloat16)
    hidden[...] = state
    wide = state.astype(jnp.float32)
    scale = lax.rsqrt(jnp.mean(wide * wide, axis=1, keepdims=True) + 1e-6)
    normed = wide * scale * gain[...]
    for piece in range(PIECES):
        rows[pl.ds(piece, TOKENS, stride=PIECES), :] = normed[:, piece * 128 : (piece + 1) * 128]

    @pl.loop(0, SLOTS // 8)
    def clear(group):
        outgoing[pl.ds(group * 8, 8)] = jnp.zeros((8, PIECES, 128), jnp.bfloat16)

    listing.wait()

    @pl.loop(0, TOKENS)
    def place(token):
        row = rows[pl.ds(pl.multiple_of(token * PIECES, PIECES), PIECES), :].astype(jnp.bfloat16)
        for choice in range(TOP):
            outgoing[slots[token, choice]] = row


def expert_kernel(
    incoming,
    w_gate,
    w_up,
    w_down,
    out,
    gate_buf,
    up_buf,
    down_buf,
    fetch_sems,
    gate,
    upward,
    wide,
    rows,
    stage,
    sems,
):
    def pair(part):
        span = pl.ds(part * 1024, 1024)
        return [
            pltpu.make_async_copy(
                w_gate.at[0, span], gate_buf.at[span], fetch_sems.at[2 * part]
            ),
            pltpu.make_async_copy(
                w_up.at[0, span], up_buf.at[span], fetch_sems.at[2 * part + 1]
            ),
        ]

    def down(part):
        return pltpu.make_async_copy(
            w_down.at[0, :, pl.ds(part * 1024, 1024)], down_buf.at[part], fetch_sems.at[8 + part]
        )

    pairs = [pair(part) for part in range(4)]
    downs = [down(part) for part in range(4)]
    for copy in pairs[0] + pairs[1] + pairs[2] + pairs[3] + downs:
        copy.start()

    @pl.loop(0, SLOTS // 32)
    def widen(group):
        wide[pl.ds(group * 32 * PIECES, 32 * PIECES), :] = incoming[
            pl.ds(group * 32 * PIECES, 32 * PIECES), :
        ].astype(jnp.float32)

    for piece in range(PIECES):
        rows[:, piece * 128 : (piece + 1) * 128] = wide[
            pl.ds(piece, SLOTS, stride=PIECES), :
        ].astype(jnp.bfloat16)
    for part in range(4):
        span = slice(part * 1024, (part + 1) * 1024)
        for copy in pairs[part]:
            copy.wait()
        for total, weights in ((gate, gate_buf), (upward, up_buf)):
            product = jnp.dot(rows[:, span], weights[span, :], preferred_element_type=jnp.float32)
            if part:
                total[...] += product
            else:
                total[...] = product
    active = (gate[...] / (1.0 + jnp.exp(-gate[...])) * upward[...]).astype(jnp.bfloat16)
    for part in range(8):
        if part % 2 == 0:
            downs[part // 2].wait()
        half = part % 2
        produced = jnp.dot(
            active,
            down_buf[part // 2, :, half * 512 : (half + 1) * 512],
            preferred_element_type=jnp.float32,
        )
        for lane in range(4):
            piece = part * 4 + lane
            for tile in range(SLOTS // 8):
                start = tile * 8 * PIECES + piece * 8
                wide[start : start + 8, :] = produced[
                    tile * 8 : (tile + 1) * 8, lane * 128 : (lane + 1) * 128
                ]
    copies = []
    for quarter in range(4):

        @pl.loop(quarter * 8, quarter * 8 + 8)
        def narrow(tile):
            for row in range(8):
                start = pl.multiple_of((tile * 8 + row) * PIECES, PIECES)
                stage[pl.ds(start, PIECES), :] = wide[
                    pl.ds(tile * 8 * PIECES + row, PIECES, stride=8), :
                ].astype(jnp.bfloat16)

        span = pl.ds(quarter * 64 * PIECES, 64 * PIECES)
        copy = pltpu.make_async_copy(stage.at[span], out.at[span], sems.at[quarter])
        copy.start()
        copies.append(copy)
    for copy in copies:
        copy.wait()


def mix_kernel(slots, weights, returned, out, rows):
    @pl.loop(0, TOKENS)
    def gather(token):
        total = jnp.zeros((PIECES, 128), jnp.float32)
        for choice in range(TOP):
            total = total + weights[token, choice] * returned[slots[token, choice]].astype(
                jnp.float32
            )
        rows[pl.ds(pl.multiple_of(token * PIECES, PIECES), PIECES), :] = total

    for piece in range(PIECES):
        out[:, piece * 128 : (piece + 1) * 128] = rows[pl.ds(piece, TOKENS, stride=PIECES), :]


def swap_cores(array):
    return lax.ppermute(array, "c", [(0, 1), (1, 0)])


def gather_blocks(block):
    fetched, handed = [], []
    for step in range(4):
        pairs = []
        for x in range(4):
            for y in range(2):
                for core in range(2):
                    target_x = (x + step) % 4
                    target_y = y if core == y else 1 - y
                    pairs.append(((x * 2 + y) * 2 + core, (target_x * 2 + target_y) * 2 + y))
        fetched.append(lax.ppermute(block, ("x", "yl", "c"), pairs))
        handed.append(swap_cores(fetched[-1]))
    x, core = lax.axis_index("x"), lax.axis_index("c")
    rings = [lax.rem(x - step + 4, 4) * 2 for step in range(4)]
    origins = [ring + core for ring in rings] + [ring + 1 - core for ring in rings]
    return fetched + handed, origins


def on_device(
    queries,
    keys,
    values,
    out_proj,
    residual,
    norm_gain,
    routes,
    route_weights,
    w_gate,
    w_up,
    w_down,
):
    ctx_index = lax.axis_index(CTX)
    core = lax.axis_index("c")
    shared_head = lax.axis_index(CHIPS) // 2
    own_keys = lax.dynamic_slice_in_dim(keys, shared_head * HEAD_WIDTH, HEAD_WIDTH, 1)
    own_values = lax.dynamic_slice_in_dim(values, shared_head * HEAD_WIDTH, HEAD_WIDTH, 1)
    blocks, origins = gather_blocks(jnp.concatenate([own_keys, own_values], axis=1))
    split = queries.reshape(8, 2, TOKENS, 256)
    own_queries = lax.dynamic_index_in_dim(split, core, 1, False).reshape(128, 256)
    sent_queries = lax.dynamic_index_in_dim(split, 1 - core, 1, False).reshape(128, 256)
    twin_queries = swap_cores(sent_queries)
    twin_proj = swap_cores(out_proj)
    sent_back, blocks[0] = lax.optimization_barrier((twin_proj, blocks[0]))
    own_proj = swap_cores(sent_back)

    slots, weights = pl.pallas_call(
        slots_kernel,
        out_shape=(
            jax.ShapeDtypeStruct((TOKENS, TOP), jnp.int32),
            jax.ShapeDtypeStruct((TOKENS, TOP), jnp.float32),
        ),
        in_specs=[SMEM, SMEM],
        out_specs=(HBM, HBM),
        scratch_shapes=[
            pltpu.SMEM((TOKENS, TOP), jnp.int32),
            pltpu.SMEM((TOKENS, TOP), jnp.float32),
            pltpu.SMEM((EXPERTS,), jnp.int32),
            pltpu.SemaphoreType.DMA((2,)),
        ],
        name="number_slots",
    )(routes, route_weights)

    place = jnp.stack([ctx_index, core] + origins).astype(jnp.int32)
    partial = pl.pallas_call(
        attention_kernel,
        out_shape=jax.ShapeDtypeStruct((128, D), jnp.bfloat16),
        in_specs=[SMEM] + [VMEM] * 10 + [HBM, HBM],
        out_specs=VMEM,
        scratch_shapes=[
            pltpu.VMEM((512, D), jnp.bfloat16),
            pltpu.SemaphoreType.DMA((2,)),
            pltpu.VMEM((512, 8 * BLOCK), jnp.float32),
            pltpu.VMEM((512, 128), jnp.float32),
            pltpu.VMEM((512, 128), jnp.float32),
            pltpu.VMEM((512, 128), jnp.float32),
            pltpu.VMEM((8, BLOCK, 256), jnp.bfloat16),
        ],
        compiler_params=pltpu.CompilerParams(vmem_limit_bytes=24 * MIB),
        name="attend_project",
    )(place, own_queries, twin_queries, *blocks, own_proj, twin_proj)

    shares = lax.all_to_all(
        partial.reshape(8, TOKENS, D), CHIPS, split_axis=0, concat_axis=0, tiled=True
    )
    hidden_state, outgoing = pl.pallas_call(
        norm_kernel,
        out_shape=(
            jax.ShapeDtypeStruct((TOKENS, D), jnp.bfloat16),
            jax.ShapeDtypeStruct((SLOTS, PIECES, 128), jnp.bfloat16),
        ),
        in_specs=[HBM, VMEM, VMEM, VMEM],
        out_specs=(VMEM, VMEM),
        scratch_shapes=[
            pltpu.VMEM((TOKENS * PIECES, 128), jnp.float32),
            pltpu.SMEM((TOKENS, TOP), jnp.int32),
            pltpu.SemaphoreType.DMA,
        ],
        compiler_params=pltpu.CompilerParams(vmem_limit_bytes=16 * MIB),
        name="norm_dispatch",
    )(slots, shares, residual, norm_gain.reshape(1, D))

    incoming = lax.all_to_all(
        outgoing.reshape(EXPERTS, CAP * PIECES, 128), ALL, split_axis=0, concat_axis=0, tiled=True
    )
    produced = pl.pallas_call(
        expert_kernel,
        out_shape=pltpu.HBM((SLOTS * PIECES, 128), jnp.bfloat16),
        in_specs=[VMEM, HBM, HBM, HBM],
        out_specs=HBM,
        scratch_shapes=[
            pltpu.VMEM((D, FF), jnp.bfloat16),
            pltpu.VMEM((D, FF), jnp.bfloat16),
            pltpu.VMEM((4, FF, 1024), jnp.bfloat16),
            pltpu.SemaphoreType.DMA((12,)),
            pltpu.VMEM((SLOTS, FF), jnp.float32),
            pltpu.VMEM((SLOTS, FF), jnp.float32),
            pltpu.VMEM((SLOTS * PIECES, 128), jnp.float32),
            pltpu.VMEM((SLOTS, D), jnp.bfloat16),
            pltpu.VMEM((SLOTS * PIECES, 128), jnp.bfloat16),
            pltpu.SemaphoreType.DMA((4,)),
        ],
        compiler_params=pltpu.CompilerParams(vmem_limit_bytes=56 * MIB),
        name="expert_rows",
    )(incoming.reshape(SLOTS * PIECES, 128), w_gate, w_up, w_down)
    returned = lax.all_to_all(
        produced.reshape(EXPERTS, CAP * PIECES, 128), ALL, split_axis=0, concat_axis=0, tiled=True
    )
    expert_mix = pl.pallas_call(
        mix_kernel,
        out_shape=jax.ShapeDtypeStruct((TOKENS, D), jnp.float32),
        in_specs=[SMEM, SMEM, VMEM],
        out_specs=VMEM,
        scratch_shapes=[pltpu.VMEM((TOKENS * PIECES, 128), jnp.float32)],
        compiler_params=pltpu.CompilerParams(vmem_limit_bytes=16 * MIB),
        name="mix",
    )(slots, weights, returned.reshape(SLOTS, PIECES, 128))
    return (hidden_state, expert_mix)


def solution(mesh):
    fine = Mesh(mesh.devices.reshape(4, 2, 2, 4, 2), ALL)
    exp = ("yh", "z", "c")
    placed = (
        P(CTX, exp),
        P(CTX, None),
        P(CTX, None),
        P(exp, None),
        P(ALL, None),
        P(),
        P(ALL, None),
        P(ALL, None),
        P(ALL, None, None),
        P(ALL, None, None),
        P(ALL, None, None),
    )
    return jax.shard_map(
        on_device,
        mesh=fine,
        in_specs=placed,
        out_specs=(P(ALL, None), P(ALL, None)),
        check_vma=False,
    )
```
